128 devices in a mesh: grp: 4 (over x), dev: 32 (over z, y, core).
Axes of the slice: x: 4, y: 4, z: 4, core: 2. Of those that a mesh axis runs over, the one named last changes fastest.
Arguments:
- flat_master: float32 [9728, 128, 128], P(('grp', 'dev')), may hold values from -2 to 2
- norm_gains: float32 [2048], P(('grp', 'dev')), may hold values from 0.1 to 1.9
- place: int32 [128, 76], replicated, may hold values from 0 to 9727, as said below
- serve_rank: int32 [128], replicated, may hold values from 0 to 127, each once
Outputs:
- qk_absorbed: bfloat16 [128, 1536, 512], P(('grp', 'dev'))
- vo_absorbed: bfloat16 [128, 512, 7168], P(('grp', 'dev'))
The draws below stay inside these ranges and needn't reach their ends.
Inputs may be any that keep to these rules, and one draw needn't show every extreme that they name: place is a permutation of all flat block indices; flat block index b lies on device b // 76; each device holds at most 1 block of any one head, so its 76 blocks belong to 76 distinct heads.
All inputs are finite; a program needn't handle non-finite values.
Results may differ from the reference program's by a relative error of at most 0.001.
Values sent between devices are 32-bit elements; how exact they have to be, the bound alone decides.
A program may use at most 128 MiB of HBM per device.

```python
import jax
import jax.numpy as jnp
from jax import lax

DH = 128
QL = 1536
KL = 512
D = 7168
HEADS = 128
BLOCKS = 76
DEVICES = 128


def draw_place(key, part):
    key = jax.random.fold_in(key, 7)
    key_head, key_block, key_slot = jax.random.split(key, 3)
    shift_head = jax.random.permutation(key_head, HEADS)
    shift_block = jax.random.permutation(key_block, BLOCKS) % HEADS
    device = (shift_head[:, None] + shift_block[None, :]) % HEADS
    slot_keys = jax.random.split(key_slot, HEADS)
    slots = jax.vmap(lambda k: jax.random.permutation(k, BLOCKS))(slot_keys)
    column = jnp.broadcast_to(jnp.arange(BLOCKS)[None, :], (HEADS, BLOCKS))
    local = slots[device, column]
    return (device * BLOCKS + local).astype(jnp.int32)


def block_scale(own_key, dims, cuts, low, largest):
    def one(position, blocks):
        heights = jax.random.uniform(jax.random.fold_in(jax.random.fold_in(own_key, 6), position), (blocks,), jnp.float32, low / len(cuts), largest / len(cuts))
        return jnp.repeat(jnp.exp(heights), dims[position] // blocks).reshape((-1,) + (1,) * (len(dims) - position - 1))

    factor_of = one(*cuts[0])
    for cut in cuts[1:]:
        factor_of = factor_of * one(*cut)
    return factor_of


def noise(key, extent, width, bound, cuts=(), kind=jnp.bfloat16):
    values = jax.random.normal(key, extent, jnp.float32) * width
    if len(cuts) > 0:
        values = block_scale(key, extent, cuts, -0.22, 0.18) * values
    return jnp.clip(values, min=-bound, max=bound).astype(kind)


def setup_inputs(seed: int = 0) -> dict:
    key_list = jax.random.split(jax.random.key(seed), 5)
    return {
        "flat_master": noise(key_list[0], (DEVICES * BLOCKS, DH, DH), 0.3, 2.0, ((0, 128),), jnp.float32),
        "norm_gains": jnp.clip(1.0 + 0.18 * jax.random.normal(key_list[1], (QL + KL,), jnp.float32), 0.1, 1.9),
        "place": draw_place(jax.random.fold_in(key_list[4], 71), 0),
        "serve_rank": jax.random.permutation(key_list[3], HEADS).astype(jnp.int32),
    }


def absorb(blocks, gain_q, gain_kv):
    qb = QL // DH
    kb = KL // DH
    w_uq = blocks[:qb].reshape(QL, DH)
    w_uk = blocks[qb:qb + kb].reshape(KL, DH)
    w_uv = blocks[qb + kb:qb + 2 * kb].reshape(KL, DH)
    w_out = blocks[qb + 2 * kb:].transpose(1, 0, 2).reshape(DH, D)
    query_key = jnp.dot(w_uq, w_uk.T, precision=lax.Precision.HIGHEST, preferred_element_type=jnp.float32)
    query_key = query_key * gain_q[:, None] * gain_kv[None, :]
    value_out = jnp.dot(w_uv, w_out, precision=lax.Precision.HIGHEST, preferred_element_type=jnp.float32)
    value_out = value_out * gain_kv[:, None]
    return query_key.astype(jnp.bfloat16), value_out.astype(jnp.bfloat16)


def reference(flat_master, norm_gains, place, serve_rank):
    gain_q = norm_gains[:QL]
    gain_kv = norm_gains[QL:QL + KL]

    def one_head(head):
        rows = place[head]
        return absorb(flat_master[rows], gain_q, gain_kv)

    query_key, value_out = lax.map(one_head, jnp.arange(HEADS, dtype=jnp.int32))
    qk_absorbed = jnp.zeros((HEADS, QL, KL), jnp.bfloat16).at[serve_rank].set(query_key)
    vo_absorbed = jnp.zeros((HEADS, KL, D), jnp.bfloat16).at[serve_rank].set(value_out)
    return qk_absorbed, vo_absorbed
```

```python
import functools

import jax
import jax.numpy as jnp
from jax import lax
from jax.experimental import pallas as pl
from jax.experimental.pallas import tpu as pltpu
from jax.sharding import PartitionSpec as P

DH = 128
QL = 1536
KL = 512
D = 7168
HEADS = 128
BLOCKS = 76
SHARE = (QL + KL) // HEADS
MESH = pl.DeviceIdType.MESH

ROUTES = ((0, 1, 2), (1, 2, 0), (2, 0, 1))
STARTS = (0, 48, 88)
ROWS = (48, 40, 40)
HOPS = (1, 3, 2)


def position():
    dev = lax.axis_index("dev")
    return (lax.axis_index("grp"), dev // 8, (dev // 2) % 4, dev % 2)


def device(coords, core):
    x, z, y = coords
    return (x, z * 8 + y * 2 + core)


def shifted(coords, dim, by):
    moved = list(coords)
    moved[dim] = (moved[dim] + by) % 4
    return moved


def exchange_kernel(
    flat_hbm, gains_ref, place_ref, serve_ref,
    got0, got1, got2, gain_out, where_out,
    flat, tab_v, tab_s, own0, own1, own2, first0, first1, first2,
    second0, second1, second2, gather, load_sem, tab_sem, send_sem, recv_sem, home_sem,
):
    x, z, y, core = position()
    here = (x, z, y)
    me = x * 32 + z * 8 + y * 2 + core
    own, first, second, got = (
        (own0, own1, own2), (first0, first1, first2), (second0, second1, second2), (got0, got1, got2))

    load = pltpu.make_async_copy(flat_hbm, flat, load_sem)
    load.start()

    barrier = pltpu.get_barrier_semaphore()
    peers = [device(here, 1 - core)]
    for dim in range(3):
        for hop in HOPS:
            for c in (core, 1 - core):
                peers.append(device(shifted(here, dim, hop), c))
    for peer in peers:
        pl.semaphore_signal(barrier, inc=1, device_id=peer, device_id_type=MESH)

    place = place_ref[...]
    local = place - me * BLOCKS
    held = (local >= 0) & (local < BLOCKS)
    block_of_head = jnp.sum(jnp.where(held, local, 0), axis=1, keepdims=True)
    rank_of_head = jnp.transpose(jnp.broadcast_to(serve_ref[...], (HEADS, HEADS)))
    target = lax.broadcasted_iota(jnp.int32, (HEADS, HEADS), 1)
    tab_v[...] = jnp.sum(
        jnp.where(rank_of_head == target, block_of_head, 0), axis=0, keepdims=True)
    table = pltpu.make_async_copy(tab_v, tab_s, tab_sem)
    table.start()
    mine = jnp.sum(
        jnp.where(rank_of_head[:, :BLOCKS] == me, place, 0), axis=0, keepdims=True)
    source = (mine * 55189) >> 22
    away = ((x - (source >> 5)) & 3, (z - (source >> 3)) & 3, (y - (source >> 1)) & 3)
    for o, (d1, d2, d3) in enumerate(ROUTES):
        slot = ((away[d3] * 2 + (source & 1)) * 4 + away[d2]) * 4 + away[d1]
        where_out[pl.ds(o, 1), pl.ds(0, BLOCKS)] = slot

    gather[me] = gains_ref[...]

    table.wait()
    load.wait()

    def pack(i, carry):
        rx, rz, ry, c = i // 32, (i // 8) % 4, (i // 2) % 4, i % 2
        to = ((x + rx) % 4) * 32 + ((z + rz) % 4) * 8 + ((y + ry) % 4) * 2 + c
        block = tab_s[0, to]
        own0[rx, rz, ry, c] = flat[block, pl.ds(STARTS[0], ROWS[0])]
        own1[rz, ry, rx, c] = flat[block, pl.ds(STARTS[1], ROWS[1])]
        own2[ry, rx, rz, c] = flat[block, pl.ds(STARTS[2], ROWS[2])]
        return carry

    lax.fori_loop(0, HEADS, pack, 0)
    pl.semaphore_wait(barrier, len(peers))

    copies = []

    def send(src, dst, to):
        n = len(copies)
        copy = pltpu.make_async_remote_copy(
            src, dst, send_sem.at[n], recv_sem.at[n], device_id=to, device_id_type=MESH)
        copy.start()
        copies.append(copy)
        return copy

    into_first = {}
    for r in HOPS:
        for o, (d1, d2, d3) in enumerate(ROUTES):
            into_first[o, r] = send(
                own[o].at[r], first[o].at[r - 1], device(shifted(here, d1, r), core))
    gain_x = [send(gather.at[me], gather.at[me], device(shifted(here, 0, r), core)) for r in HOPS]
    into_second = {}
    for r in HOPS:
        for o, (d1, d2, d3) in enumerate(ROUTES):
            into_second[o, r, 0] = send(
                own[o].at[0, r], second[o].at[r - 1, 0], device(shifted(here, d2, r), core))

    for q in HOPS:
        for o, (d1, d2, d3) in enumerate(ROUTES):
            into_first[o, q].wait_recv()
            for r in HOPS:
                into_second[o, r, q] = send(
                    first[o].at[q - 1, r], second[o].at[r - 1, q],
                    device(shifted(here, d2, r), core))

    for copy in gain_x:
        copy.wait_recv()
    rows = [((x + k) % 4) * 32 + z * 8 + y * 2 + core for k in range(4)]
    gain_z = [
        send(gather.at[row], gather.at[row], device(shifted(here, 1, r), core))
        for r in HOPS for row in rows]

    final = []
    homes = []

    def deliver(o, src, dst_index):
        d3 = ROUTES[o][2]
        for r in (1, 3, 2, 0):
            for c in range(2):
                to_core = core if c == 0 else 1 - core
                a, b = src(r, to_core), got[o].at[(r, core) + dst_index]
                if r == 0 and c == 0:
                    copy = pltpu.make_async_copy(a, b, home_sem.at[len(homes)])
                    copy.start()
                    homes.append(copy)
                else:
                    final.append(send(a, b, device(shifted(here, d3, r), to_core)))

    for o in range(3):
        deliver(o, lambda r, c: own[o].at[0, 0, r, c], (0, 0))
        deliver(o, lambda r, c: first[o].at[:, 0, r, c], (0, pl.ds(1, 3)))

    for copy in gain_z:
        copy.wait_recv()
    gain_y = []
    for k in range(4):
        for l in range(4):
            row = ((x + k) % 4) * 32 + ((z + l) % 4) * 8 + y * 2 + core
            for r in (1, 3, 2, 0):
                for c in (core, 1 - core):
                    if r == 0 and c is core:
                        continue
                    gain_y.append(send(
                        gather.at[row], gather.at[row], device(shifted(here, 2, r), c)))

    for q in HOPS:
        for o in range(3):
            for r1 in range(4):
                into_second[o, q, r1].wait_recv()
            deliver(o, lambda r, c: second[o].at[q - 1, :, r, c], (q,))

    for copy in gain_y:
        copy.wait_recv()
    turned = jnp.transpose(gather[...].reshape(HEADS, HEADS))
    for d in range(HEADS):
        gain_out[pl.ds(d * SHARE, SHARE)] = jnp.broadcast_to(
            turned[:SHARE, d:d + 1], (SHARE, DH))

    for copy in final:
        copy.wait_recv()
    for copy in homes:
        copy.wait()
    for copy in copies:
        copy.wait_send()


def exchange(flat_master, gains, place, serve_rank):
    def parts(*lead):
        return [pltpu.VMEM(lead + (n, DH), jnp.float32) for n in ROWS]

    n_sends = 9 + 3 + 9 + 27 + 12 + 3 * 7 * 5 + 112
    return pl.pallas_call(
        exchange_kernel,
        out_shape=[jax.ShapeDtypeStruct((4, 2, 4, 4, n, DH), jnp.float32) for n in ROWS] + [
            jax.ShapeDtypeStruct((QL + KL, DH), jnp.float32),
            jax.ShapeDtypeStruct((8, 128), jnp.int32)],
        in_specs=[pl.BlockSpec(memory_space=pl.ANY)] + [pl.BlockSpec(memory_space=pltpu.VMEM)] * 3,
        out_specs=[pl.BlockSpec(memory_space=pl.ANY)] * 3 + [pl.BlockSpec(memory_space=pltpu.VMEM)] * 2,
        scratch_shapes=[
            pltpu.VMEM((BLOCKS, DH, DH), jnp.float32),
            pltpu.VMEM((1, HEADS), jnp.int32),
            pltpu.SMEM((1, HEADS), jnp.int32),
            *parts(4, 4, 4, 2), *parts(3, 4, 4, 2), *parts(3, 4, 4, 2),
            pltpu.VMEM((HEADS, 1, DH), jnp.float32),
            pltpu.SemaphoreType.DMA,
            pltpu.SemaphoreType.DMA,
            pltpu.SemaphoreType.DMA((n_sends,)),
            pltpu.SemaphoreType.DMA((n_sends,)),
            pltpu.SemaphoreType.DMA((15,)),
        ],
        compiler_params=pltpu.CompilerParams(
            collective_id=0, has_side_effects=True, vmem_limit_bytes=56 << 20),
        name="exchange",
    )(flat_master, gains, place, serve_rank)


def split(a):
    high = a.astype(jnp.bfloat16)
    return high, (a - high.astype(jnp.float32)).astype(jnp.bfloat16)


def product_kernel(where, got0, got1, got2, gain, qk_ref, vo_ref, uv, uk_high, uk_low):
    step = pl.program_id(0)

    def block(j):
        return jnp.concatenate(
            [got[where[o, j]] for o, got in enumerate((got0, got1, got2))], axis=0)

    @pl.when(step == 0)
    def _():
        for b in range(KL // DH):
            g = gain[pl.ds(QL + b * DH, DH)]
            high, low = split(block(QL // DH + b) * g)
            uk_high[pl.ds(b * DH, DH)] = jnp.concatenate([high, high], axis=1)
            uk_low[pl.ds(b * DH, DH)] = jnp.concatenate([low, low], axis=1)
            high, low = split(block((QL + KL) // DH + b) * g)
            uv[pl.ds(b * DH, DH)] = jnp.concatenate([high, low], axis=1)

    @pl.when(step < 6)
    def _():
        for b in range(2):
            j = step * 2 + b
            g = gain[pl.ds(pl.multiple_of(j * DH, DH), DH)]
            left = jnp.concatenate(split(block(j) * g), axis=1)
            dims = (((1,), (1,)), ((), ()))
            out = lax.dot_general(left, uk_high[...], dims, preferred_element_type=jnp.float32)
            out += lax.dot_general(left, uk_low[...], dims, preferred_element_type=jnp.float32)
            qk_ref[0, pl.ds(b * DH, DH)] = out.astype(jnp.bfloat16)

    for b in range(4):
        parts = [split(block((QL + 2 * KL) // DH + step * 8 + b * 2 + k)) for k in range(2)]
        high = jnp.concatenate([parts[0][0], parts[1][0]], axis=1)
        low = jnp.concatenate([parts[0][1], parts[1][1]], axis=1)
        out = jnp.dot(uv[...], jnp.concatenate([high, high], axis=0), preferred_element_type=jnp.float32)
        out += jnp.dot(uv[...], jnp.concatenate([low, low], axis=0), preferred_element_type=jnp.float32)
        vo_ref[0, :, pl.ds(b * 256, 256)] = out.astype(jnp.bfloat16)


def products(where, got, gain):
    return pl.pallas_call(
        product_kernel,
        grid_spec=pltpu.PrefetchScalarGridSpec(
            num_scalar_prefetch=1,
            grid=(7,),
            in_specs=[pl.BlockSpec(memory_space=pltpu.VMEM)] * 4,
            out_specs=[
                pl.BlockSpec((1, 256, KL), lambda i, w: (0, jnp.minimum(i, 5), 0)),
                pl.BlockSpec((1, KL, 1024), lambda i, w: (0, 0, i))],
            scratch_shapes=[pltpu.VMEM((KL, 2 * DH), jnp.bfloat16)] * 3,
        ),
        out_shape=[
            jax.ShapeDtypeStruct((1, QL, KL), jnp.bfloat16),
            jax.ShapeDtypeStruct((1, KL, D), jnp.bfloat16)],
        compiler_params=pltpu.CompilerParams(vmem_limit_bytes=56 << 20),
        name="products",
    )(where, *got, gain)


def body(flat_master, norm_gains, place, serve_rank):
    gains = jnp.pad(norm_gains[None], ((0, 0), (0, DH - SHARE)))
    *got, gain, where = exchange(flat_master, gains, place, serve_rank[None])
    got = [g.reshape(HEADS, n, DH) for g, n in zip(got, ROWS)]
    return tuple(products(where, got, gain))


def solution(mesh):
    in_specs = (P(("grp", "dev"), None, None), P(("grp", "dev")), P(), P())
    out_specs = (P(("grp", "dev"), None, None), P(("grp", "dev"), None, None))
    return jax.shard_map(body, mesh=mesh, in_specs=in_specs, out_specs=out_specs, check_vma=False)
```

```python
import jax
import jax.numpy as jnp
from jax import lax
from jax.experimental import pallas as pl
from jax.experimental.pallas import tpu as pltpu
from jax.sharding import PartitionSpec as P

DH = 128
QL = 1536
KL = 512
D = 7168
HEADS = 128
BLOCKS = 76
SHARE = (QL + KL) // HEADS
STRIP = 512
MESH = pl.DeviceIdType.MESH

ROUTES = ((0, 1, 2), (1, 2, 0), (2, 0, 1))
STARTS = (0, 48, 88)
ROWS = (48, 40, 40)
HOPS = (1, 3, 2)


def position():
    dev = lax.axis_index("dev")
    return (lax.axis_index("grp"), dev // 8, (dev // 2) % 4, dev % 2)


def device(coords, core):
    x, z, y = coords
    return (x, z * 8 + y * 2 + core)


def shifted(coords, dim, by):
    moved = list(coords)
    moved[dim] = (moved[dim] + by) % 4
    return moved


def exchange_kernel(
    flat_hbm, gains_hbm, place_hbm, serve_hbm,
    got0, got1, got2, gain_out, where_out,
    flat, gains_ref, place_ref, serve_ref, tab_v, tab_s,
    own0, own1, own2, first0, first1, first2, second0, second1, second2, gather,
    load_sem, tab_sem, first_sem, second_sem, got_sem, gain_sem,
    sent_first, sent_second, sent_got, sent_core, sent_gain,
):
    x, z, y, core = position()
    here = (x, z, y)
    me = x * 32 + z * 8 + y * 2 + core
    own, first, second, got = (
        (own0, own1, own2), (first0, first1, first2), (second0, second1, second2), (got0, got1, got2))

    loads = [
        pltpu.make_async_copy(src, dst, load_sem.at[n]) for n, (src, dst) in enumerate((
            (place_hbm, place_ref), (serve_hbm, serve_ref), (gains_hbm, gains_ref),
            (flat_hbm, flat)))]
    for load in loads:
        load.start()

    barrier = pltpu.get_barrier_semaphore()
    peers = [device(here, 1 - core)]
    for dim in range(3):
        for hop in HOPS:
            for c in (core, 1 - core):
                peers.append(device(shifted(here, dim, hop), c))
    for peer in peers:
        pl.semaphore_signal(barrier, inc=1, device_id=peer, device_id_type=MESH)

    for load in loads[:3]:
        load.wait()
    place = place_ref[...]
    local = place - me * BLOCKS
    held = (local >= 0) & (local < BLOCKS)
    block_of_head = jnp.sum(jnp.where(held, local, 0), axis=0, keepdims=True)
    pairs = jnp.broadcast_to(serve_ref[...] * 128 + block_of_head, (HEADS, HEADS))
    pairs = jnp.transpose(pairs)
    target = lax.broadcasted_iota(jnp.int32, (HEADS, HEADS), 1)
    tab_v[...] = jnp.sum(
        jnp.where(pairs >> 7 == target, pairs & 127, 0), axis=0, keepdims=True)
    table = pltpu.make_async_copy(tab_v, tab_s, tab_sem)
    table.start()
    gather[x, z, y, core] = jnp.concatenate(
        [gains_ref[...], jnp.zeros((1, DH - SHARE), jnp.float32)], axis=1)
    table.wait()
    loads[3].wait()
    pl.semaphore_wait(barrier, len(peers))

    def pack(o, r):
        d1, d2, d3 = ROUTES[o]
        dst = own[o].at[r - 1] if r else first[o].at[0]

        def one(i, carry):
            a, b, c = i // 8, (i // 2) % 4, i % 2
            to = [None] * 3
            to[d1], to[d2], to[d3] = (here[d1] + r) % 4, (here[d2] + a) % 4, (here[d3] + b) % 4
            block = tab_s[0, to[0] * 32 + to[1] * 8 + to[2] * 2 + c]
            dst[a, b, c] = flat[block, pl.ds(STARTS[o], ROWS[o])]
            return carry

        lax.fori_loop(0, 32, one, 0, unroll=8)

    def send(src, dst, sent, landed, to):
        pltpu.make_async_remote_copy(
            src, dst, sent, landed, device_id=to, device_id_type=MESH).start()

    def await_bytes(ref, sem):
        pltpu.make_async_copy(ref, ref, sem).wait()

    for r in HOPS:
        for o, (d1, d2, d3) in enumerate(ROUTES):
            pack(o, r)
            send(own[o].at[r - 1], first[o].at[r], sent_first.at[o], first_sem.at[o, r - 1],
                 device(shifted(here, d1, r), core))
    mine = gather.at[x, z, y, core]
    for r in HOPS:
        send(mine, mine, sent_gain.at[0], gain_sem.at[0], device(shifted(here, 0, r), core))

    def forward(o, q):
        d2 = ROUTES[o][1]
        for r in HOPS:
            send(first[o].at[q, r], second[o].at[r - 1, q], sent_second.at[o],
                 second_sem.at[o, r - 1], device(shifted(here, d2, r), core))

    for o in range(3):
        pack(o, 0)
        forward(o, 0)

    wanted = jnp.sum(jnp.where(serve_ref[...] == me, place_ref[...], 0), axis=1, keepdims=True)
    wanted = jnp.transpose(jnp.broadcast_to(wanted, (BLOCKS, HEADS)))[:1]
    source = (wanted * 55189) >> 22
    away = ((x - (source >> 5)) & 3, (z - (source >> 3)) & 3, (y - (source >> 1)) & 3)
    for o, (d1, d2, d3) in enumerate(ROUTES):
        slot = ((away[d3] * 2 + (source & 1)) * 4 + away[d2]) * 4 + away[d1]
        where_out[pl.ds(o, 1), pl.ds(0, BLOCKS)] = slot

    for q in HOPS:
        for o in range(3):
            await_bytes(first[o].at[q], first_sem.at[o, q - 1])
            forward(o, q)

    await_bytes(gather.at[0, 0, pl.ds(0, 3), 0], gain_sem.at[0])
    mine = gather.at[:, z, y, core]
    for r in HOPS:
        send(mine, mine, sent_gain.at[1], gain_sem.at[1], device(shifted(here, 1, r), core))

    def deliver(o, src, q):
        d3 = ROUTES[o][2]
        for r in (1, 3, 2, 0):
            for c in (0, 1):
                to_core = (core + c) % 2
                a, b = src.at[:, r, to_core], got[o].at[r, core, q]
                if r == 0 and c == 0:
                    pltpu.make_async_copy(a, b, got_sem.at[o]).start()
                else:
                    send(a, b, sent_got.at[o] if r else sent_core.at[o], got_sem.at[o],
                         device(shifted(here, d3, r), to_core))

    for o in range(3):
        deliver(o, first[o].at[:, 0], 0)

    await_bytes(gather.at[pl.ds(0, 3), 0, :, 0], gain_sem.at[1])
    mine = gather.at[:, :, y, core]
    for r in (1, 3, 2, 0):
        for c in (0, 1):
            if r or c:
                n = 2 if r else 3
                send(mine, mine, sent_gain.at[n], gain_sem.at[n],
                     device(shifted(here, 2, r), (core + c) % 2))

    for q in HOPS:
        for o in range(3):
            await_bytes(second[o].at[q - 1], second_sem.at[o, q - 1])
            deliver(o, second[o].at[q - 1], q)

    rest = gather.at[:, :, pl.ds(0, 3)]
    await_bytes(rest, gain_sem.at[2])
    await_bytes(gather.at[:, :, 3, 0], gain_sem.at[3])
    turned = jnp.transpose(gather[...].reshape(HEADS, HEADS))
    for d in range(HEADS):
        gain_out[pl.ds(d * SHARE, SHARE)] = jnp.broadcast_to(
            turned[:SHARE, d:d + 1], (SHARE, DH))

    for o in range(3):
        await_bytes(got[o], got_sem.at[o])
    for o in range(3):
        await_bytes(first[o].at[pl.ds(1, 3)], sent_first.at[o])
        await_bytes(second[o], sent_second.at[o])
        await_bytes(got[o].at[pl.ds(1, 3)], sent_got.at[o])
        await_bytes(got[o].at[0, 0], sent_core.at[o])
    await_bytes(gather.at[0, 0, pl.ds(0, 3), 0], sent_gain.at[0])
    await_bytes(gather.at[pl.ds(0, 3), 0, :, 0], sent_gain.at[1])
    await_bytes(rest, sent_gain.at[2])
    await_bytes(gather.at[:, :, 3, 0], sent_gain.at[3])


def exchange(flat_master, gains, place, serve_rank):
    def parts(*lead):
        return [pltpu.VMEM(lead + (n, DH), jnp.float32) for n in ROWS]

    dma = pltpu.SemaphoreType.DMA
    return pl.pallas_call(
        exchange_kernel,
        out_shape=parts(4, 2, 4, 4) + [
            pltpu.VMEM((QL + KL, DH), jnp.float32),
            pltpu.VMEM((8, 128), jnp.int32)],
        in_specs=[pl.BlockSpec(memory_space=pltpu.HBM)] * 4,
        out_specs=[pl.BlockSpec(memory_space=pltpu.VMEM)] * 5,
        scratch_shapes=[
            pltpu.VMEM((BLOCKS, DH, DH), jnp.float32),
            pltpu.VMEM((1, SHARE), jnp.float32),
            pltpu.VMEM((BLOCKS, HEADS), jnp.int32),
            pltpu.VMEM((1, HEADS), jnp.int32),
            pltpu.VMEM((1, HEADS), jnp.int32),
            pltpu.SMEM((1, HEADS), jnp.int32),
            *parts(3, 4, 4, 2), *parts(4, 4, 4, 2), *parts(3, 4, 4, 2),
            pltpu.VMEM((4, 4, 4, 2, 1, DH), jnp.float32),
            dma((4,)), dma, dma((3, 3)), dma((3, 3)), dma((3,)), dma((4,)),
            dma((3,)), dma((3,)), dma((3,)), dma((3,)), dma((4,)),
        ],
        compiler_params=pltpu.CompilerParams(
            collective_id=0, has_side_effects=True, vmem_limit_bytes=52 << 20),
        name="exchange",
    )(flat_master, gains, place, serve_rank)


def split(a):
    high = a.astype(jnp.bfloat16)
    return high, (a - high.astype(jnp.float32)).astype(jnp.bfloat16)


def product_kernel(where, got0, got1, got2, gain, qk_hbm, vo_hbm, uv, uk, qk, vo, sems):
    def block(j):
        return jnp.concatenate(
            [got[where[o, j]] for o, got in enumerate((got0, got1, got2))], axis=0)

    copies = []

    def write(src, dst):
        copy = pltpu.make_async_copy(src, dst, sems.at[len(copies)])
        copy.start()
        copies.append(copy)

    for b in range(KL // DH):
        rows = pl.ds(b * DH, DH)
        g = gain[pl.ds(QL + b * DH, DH)]
        high, low = split(block((QL + KL) // DH + b) * g)
        uv[rows] = jnp.concatenate([high, low, high], axis=1)
        high, low = split(jnp.transpose(block(QL // DH + b) * g))
        uk[:, rows] = jnp.concatenate([high, high, low], axis=0)

    for start in range(0, D, STRIP):
        for column in range(start, start + STRIP, 2 * DH):
            j = (QL + 2 * KL + column) // DH
            (high0, low0), (high1, low1) = split(block(j)), split(block(j + 1))
            high = jnp.concatenate([high0, high1], axis=1)
            low = jnp.concatenate([low0, low1], axis=1)
            out = jnp.dot(
                uv[...], jnp.concatenate([high, high, low], axis=0),
                preferred_element_type=jnp.float32)
            vo[:, pl.ds(column, 2 * DH)] = out.astype(jnp.bfloat16)
        strip = pl.ds(start, STRIP)
        write(vo.at[:, strip], vo_hbm.at[0, :, strip])

    for start in range(0, QL, KL):
        left = []
        for row in range(start, start + KL, DH):
            high, low = split(block(row // DH) * gain[pl.ds(row, DH)])
            left.append(jnp.concatenate([high, low, high], axis=1))
        left = jnp.concatenate(left, axis=0)
        rows = pl.ds(start, KL)
        for column in range(0, KL, 2 * DH):
            out = jnp.dot(
                left, uk[:, pl.ds(column, 2 * DH)], preferred_element_type=jnp.float32)
            qk[rows, pl.ds(column, 2 * DH)] = out.astype(jnp.bfloat16)
        write(qk.at[rows], qk_hbm.at[0, rows])

    for copy in copies:
        copy.wait()


def products(where, got, gain):
    return pl.pallas_call(
        product_kernel,
        in_specs=[pl.BlockSpec(memory_space=pltpu.SMEM)]
        + [pl.BlockSpec(memory_space=pltpu.VMEM)] * 4,
        out_specs=[pl.BlockSpec(memory_space=pl.ANY)] * 2,
        scratch_shapes=[
            pltpu.VMEM((KL, 3 * DH), jnp.bfloat16),
            pltpu.VMEM((3 * DH, KL), jnp.bfloat16),
            pltpu.VMEM((QL, KL), jnp.bfloat16),
            pltpu.VMEM((KL, D), jnp.bfloat16),
            pltpu.SemaphoreType.DMA((D // STRIP + QL // KL,)),
        ],
        out_shape=[
            jax.ShapeDtypeStruct((1, QL, KL), jnp.bfloat16),
            jax.ShapeDtypeStruct((1, KL, D), jnp.bfloat16)],
        compiler_params=pltpu.CompilerParams(vmem_limit_bytes=32 << 20),
        name="products",
    )(where, *got, gain)


def body(flat_master, norm_gains, place, serve_rank):
    *got, gain, where = exchange(flat_master, norm_gains[None], place.T, serve_rank[None])
    got = [g.reshape(HEADS, n, DH) for g, n in zip(got, ROWS)]
    return tuple(products(where, got, gain))


def solution(mesh):
    in_specs = (P(("grp", "dev"), None, None), P(("grp", "dev")), P(), P())
    out_specs = (P(("grp", "dev"), None, None), P(("grp", "dev"), None, None))
    return jax.shard_map(body, mesh=mesh, in_specs=in_specs, out_specs=out_specs, check_vma=False)
```

```python
import jax
import jax.numpy as jnp
from jax import lax
from jax.experimental import pallas as pl
from jax.experimental.pallas import tpu as pltpu
from jax.sharding import PartitionSpec as P

DH = 128
QL = 1536
KL = 512
D = 7168
HEADS = 128
BLOCKS = 76
SHARE = (QL + KL) // HEADS
STRIP = 512
PIECE = 19
MESH = pl.DeviceIdType.MESH

ROUTES = ((0, 1, 2), (1, 2, 0), (2, 0, 1))
STARTS = (0, 48, 88)
ROWS = (48, 40, 40)
HOPS = (1, 3, 2)


def position():
    dev = lax.axis_index("dev")
    return (lax.axis_index("grp"), dev // 8, (dev // 2) % 4, dev % 2)


def device(coords, core):
    x, z, y = coords
    return (x, z * 8 + y * 2 + core)


def shifted(coords, dim, by):
    moved = list(coords)
    moved[dim] = (moved[dim] + by) % 4
    return moved


def exchange_kernel(
    flat_hbm, gains_hbm, place_hbm, serve_hbm,
    got0, got1, got2, gain_out, where_out,
    gain, where, flat, gains_ref, place_ref, serve_ref, tab_v, tab_s,
    own0, own1, own2, first0, first1, first2, second0, second1, second2, gather,
    load_sem, tab_sem, out_sem, first_sem, second_sem, got_sem, gain_sem,
    sent_first, sent_second, sent_got, sent_core, sent_gain,
):
    x, z, y, core = position()
    here = (x, z, y)
    me = x * 32 + z * 8 + y * 2 + core
    own, first, second, got = (
        (own0, own1, own2), (first0, first1, first2), (second0, second1, second2), (got0, got1, got2))

    loads = [
        pltpu.make_async_copy(src, dst, load_sem.at[n]) for n, (src, dst) in enumerate((
            (place_hbm, place_ref), (serve_hbm, serve_ref), (gains_hbm, gains_ref)) + tuple(
            (flat_hbm.at[pl.ds(start, PIECE)], flat.at[pl.ds(start, PIECE)])
            for start in range(0, BLOCKS, PIECE)))]
    for load in loads:
        load.start()

    barrier = pltpu.get_barrier_semaphore()
    peers = [device(here, 1 - core)]
    for dim in range(3):
        for hop in HOPS:
            for c in (core, 1 - core):
                peers.append(device(shifted(here, dim, hop), c))
    for peer in peers:
        pl.semaphore_signal(barrier, inc=1, device_id=peer, device_id_type=MESH)

    for load in loads[:3]:
        load.wait()
    place = place_ref[...]
    local = place - me * BLOCKS
    held = (local >= 0) & (local < BLOCKS)
    block_of_head = jnp.sum(jnp.where(held, local, 0), axis=0, keepdims=True)
    pairs = jnp.broadcast_to(serve_ref[...] * 128 + block_of_head, (HEADS, HEADS))
    pairs = jnp.transpose(pairs)
    target = lax.broadcasted_iota(jnp.int32, (HEADS, HEADS), 1)
    tab_v[...] = jnp.sum(
        jnp.where(pairs >> 7 == target, pairs & 127, 0), axis=0, keepdims=True)
    table = pltpu.make_async_copy(tab_v, tab_s, tab_sem)
    table.start()
    gather[x, z, y, core] = jnp.concatenate(
        [gains_ref[...], jnp.zeros((1, DH - SHARE), jnp.float32)], axis=1)
    table.wait()
    for load in loads[3:]:
        load.wait()

    def pack(o, r):
        d1, d2, d3 = ROUTES[o]
        dst = own[o].at[r - 1] if r else first[o].at[0]

        def one(i, carry):
            a, b, c = i // 8, (i // 2) % 4, i % 2
            to = [None] * 3
            to[d1], to[d2], to[d3] = (here[d1] + r) % 4, (here[d2] + a) % 4, (here[d3] + b) % 4
            block = tab_s[0, to[0] * 32 + to[1] * 8 + to[2] * 2 + c]
            dst[a, b, c] = flat[block, pl.ds(STARTS[o], ROWS[o])]
            return carry

        lax.fori_loop(0, 32, one, 0, unroll=8)

    def send(src, dst, sent, landed, to):
        pltpu.make_async_remote_copy(
            src, dst, sent, landed, device_id=to, device_id_type=MESH).start()

    def await_bytes(ref, sem):
        pltpu.make_async_copy(ref, ref, sem).wait()

    for o in range(3):
        pack(o, HOPS[0])
    pl.semaphore_wait(barrier, len(peers))
    for r in HOPS:
        for o, (d1, d2, d3) in enumerate(ROUTES):
            if r != HOPS[0]:
                pack(o, r)
            send(own[o].at[r - 1], first[o].at[r], sent_first.at[o], first_sem.at[o, r - 1],
                 device(shifted(here, d1, r), core))
    mine = gather.at[x, z, y, core]
    for r in HOPS:
        send(mine, mine, sent_gain.at[0], gain_sem.at[0], device(shifted(here, 0, r), core))

    def forward(o, q):
        d2 = ROUTES[o][1]
        for r in HOPS:
            send(first[o].at[q, r], second[o].at[r - 1, q], sent_second.at[o],
                 second_sem.at[o, r - 1], device(shifted(here, d2, r), core))

    for o in range(3):
        pack(o, 0)
        forward(o, 0)

    wanted = jnp.sum(jnp.where(serve_ref[...] == me, place_ref[...], 0), axis=1, keepdims=True)
    wanted = jnp.transpose(jnp.broadcast_to(wanted, (BLOCKS, HEADS)))[:1]
    source = (wanted * 55189) >> 22
    away = ((x - (source >> 5)) & 3, (z - (source >> 3)) & 3, (y - (source >> 1)) & 3)
    for o, (d1, d2, d3) in enumerate(ROUTES):
        slot = ((away[d3] * 2 + (source & 1)) * 4 + away[d2]) * 4 + away[d1]
        where[pl.ds(o, 1), pl.ds(0, BLOCKS)] = slot
    where_copy = pltpu.make_async_copy(where, where_out, out_sem.at[0])
    where_copy.start()

    for q in HOPS:
        for o in range(3):
            await_bytes(first[o].at[q], first_sem.at[o, q - 1])
            forward(o, q)

    await_bytes(gather.at[0, 0, pl.ds(0, 3), 0], gain_sem.at[0])
    mine = gather.at[:, z, y, core]
    for r in HOPS:
        send(mine, mine, sent_gain.at[1], gain_sem.at[1], device(shifted(here, 1, r), core))

    def deliver(o, src, q):
        d3 = ROUTES[o][2]
        for r in (1, 3, 2, 0):
            for c in (0, 1):
                to_core = (core + c) % 2
                a, b = src.at[:, r, to_core], got[o].at[r, core, q]
                if r == 0 and c == 0:
                    pltpu.make_async_copy(a, b, got_sem.at[o]).start()
                else:
                    send(a, b, sent_got.at[o] if r else sent_core.at[o], got_sem.at[o],
                         device(shifted(here, d3, r), to_core))

    for o in range(3):
        deliver(o, first[o].at[:, 0], 0)

    await_bytes(gather.at[pl.ds(0, 3), 0, :, 0], gain_sem.at[1])
    mine = gather.at[:, :, y, core]
    for r in (1, 3, 2, 0):
        for c in (0, 1):
            if r or c:
                n = 2 if r else 3
                send(mine, mine, sent_gain.at[n], gain_sem.at[n],
                     device(shifted(here, 2, r), (core + c) % 2))

    def finish(q):
        for o in range(3):
            await_bytes(second[o].at[q - 1], second_sem.at[o, q - 1])
            deliver(o, second[o].at[q - 1], q)

    finish(HOPS[0])
    finish(HOPS[1])
    rest = gather.at[:, :, pl.ds(0, 3)]
    await_bytes(rest, gain_sem.at[2])
    await_bytes(gather.at[:, :, 3, 0], gain_sem.at[3])
    turned = jnp.transpose(gather[...].reshape(HEADS, HEADS))
    for d in range(HEADS):
        gain[pl.ds(d * SHARE, SHARE)] = jnp.broadcast_to(
            turned[:SHARE, d:d + 1], (SHARE, DH))
    gain_copy = pltpu.make_async_copy(gain, gain_out, out_sem.at[1])
    gain_copy.start()
    finish(HOPS[2])

    where_copy.wait()
    gain_copy.wait()
    for o in range(3):
        await_bytes(got[o], got_sem.at[o])
    for o in range(3):
        await_bytes(first[o].at[pl.ds(1, 3)], sent_first.at[o])
        await_bytes(second[o], sent_second.at[o])
        await_bytes(got[o].at[pl.ds(1, 3)], sent_got.at[o])
        await_bytes(got[o].at[0, 0], sent_core.at[o])
    await_bytes(gather.at[0, 0, pl.ds(0, 3), 0], sent_gain.at[0])
    await_bytes(gather.at[pl.ds(0, 3), 0, :, 0], sent_gain.at[1])
    await_bytes(rest, sent_gain.at[2])
    await_bytes(gather.at[:, :, 3, 0], sent_gain.at[3])


def exchange(flat_master, gains, place, serve_rank):
    def parts(*lead):
        return [pltpu.VMEM(lead + (n, DH), jnp.float32) for n in ROWS]

    dma = pltpu.SemaphoreType.DMA
    return pl.pallas_call(
        exchange_kernel,
        out_shape=parts(4, 2, 4, 4) + [
            pltpu.VMEM((QL + KL, DH), jnp.float32),
            pltpu.VMEM((8, 128), jnp.int32)],
        in_specs=[pl.BlockSpec(memory_space=pltpu.HBM)] * 4,
        out_specs=[pl.BlockSpec(memory_space=pl.ANY)] * 5,
        scratch_shapes=[
            pltpu.VMEM((QL + KL, DH), jnp.float32),
            pltpu.VMEM((8, 128), jnp.int32),
            pltpu.VMEM((BLOCKS, DH, DH), jnp.float32),
            pltpu.VMEM((1, SHARE), jnp.float32),
            pltpu.VMEM((BLOCKS, HEADS), jnp.int32),
            pltpu.VMEM((1, HEADS), jnp.int32),
            pltpu.VMEM((1, HEADS), jnp.int32),
            pltpu.SMEM((1, HEADS), jnp.int32),
            *parts(3, 4, 4, 2), *parts(4, 4, 4, 2), *parts(3, 4, 4, 2),
            pltpu.VMEM((4, 4, 4, 2, 1, DH), jnp.float32),
            dma((3 + BLOCKS // PIECE,)), dma, dma((2,)), dma((3, 3)), dma((3, 3)), dma((3,)), dma((4,)),
            dma((3,)), dma((3,)), dma((3,)), dma((3,)), dma((4,)),
        ],
        compiler_params=pltpu.CompilerParams(
            collective_id=0, has_side_effects=True, vmem_limit_bytes=52 << 20),
        name="exchange",
    )(flat_master, gains, place, serve_rank)


def split(a):
    high = a.astype(jnp.bfloat16)
    return high, (a - high.astype(jnp.float32)).astype(jnp.bfloat16)


def product_kernel(where, got0, got1, got2, gain, qk_hbm, vo_hbm, uv, uk, qk, vo, sems):
    def block(j):
        return jnp.concatenate(
            [got[where[o, j]] for o, got in enumerate((got0, got1, got2))], axis=0)

    copies = []

    def write(src, dst):
        copy = pltpu.make_async_copy(src, dst, sems.at[len(copies)])
        copy.start()
        copies.append(copy)

    for b in range(KL // DH):
        rows = pl.ds(b * DH, DH)
        g = gain[pl.ds(QL + b * DH, DH)]
        high, low = split(block((QL + KL) // DH + b) * g)
        uv[rows] = jnp.concatenate([high, low, high], axis=1)
        high, low = split(jnp.transpose(block(QL // DH + b) * g))
        uk[:, rows] = jnp.concatenate([high, high, low], axis=0)

    for start in range(0, D, STRIP):
        for column in range(start, start + STRIP, 2 * DH):
            j = (QL + 2 * KL + column) // DH
            (high0, low0), (high1, low1) = split(block(j)), split(block(j + 1))
            high = jnp.concatenate([high0, high1], axis=1)
            low = jnp.concatenate([low0, low1], axis=1)
            out = jnp.dot(
                uv[...], jnp.concatenate([high, high, low], axis=0),
                preferred_element_type=jnp.float32)
            vo[:, pl.ds(column, 2 * DH)] = out.astype(jnp.bfloat16)
        strip = pl.ds(start, STRIP)
        write(vo.at[:, strip], vo_hbm.at[0, :, strip])

    for start in range(0, QL, KL):
        left = []
        for row in range(start, start + KL, DH):
            high, low = split(block(row // DH) * gain[pl.ds(row, DH)])
            left.append(jnp.concatenate([high, low, high], axis=1))
        left = jnp.concatenate(left, axis=0)
        rows = pl.ds(start, KL)
        for column in range(0, KL, 2 * DH):
            out = jnp.dot(
                left, uk[:, pl.ds(column, 2 * DH)], preferred_element_type=jnp.float32)
            qk[rows, pl.ds(column, 2 * DH)] = out.astype(jnp.bfloat16)
        write(qk.at[rows], qk_hbm.at[0, rows])

    for copy in copies:
        copy.wait()


def products(where, got, gain):
    return pl.pallas_call(
        product_kernel,
        in_specs=[pl.BlockSpec(memory_space=pltpu.SMEM)]
        + [pl.BlockSpec(memory_space=pltpu.VMEM)] * 4,
        out_specs=[pl.BlockSpec(memory_space=pl.ANY)] * 2,
        scratch_shapes=[
            pltpu.VMEM((KL, 3 * DH), jnp.bfloat16),
            pltpu.VMEM((3 * DH, KL), jnp.bfloat16),
            pltpu.VMEM((QL, KL), jnp.bfloat16),
            pltpu.VMEM((KL, D), jnp.bfloat16),
            pltpu.SemaphoreType.DMA((D // STRIP + QL // KL,)),
        ],
        out_shape=[
            jax.ShapeDtypeStruct((1, QL, KL), jnp.bfloat16),
            jax.ShapeDtypeStruct((1, KL, D), jnp.bfloat16)],
        compiler_params=pltpu.CompilerParams(vmem_limit_bytes=32 << 20),
        name="products",
    )(where, *got, gain)


def body(flat_master, norm_gains, place, serve_rank):
    *got, gain, where = exchange(flat_master, norm_gains[None], place.T, serve_rank[None])
    got = [g.reshape(HEADS, n, DH) for g, n in zip(got, ROWS)]
    return tuple(products(where, got, gain))


def solution(mesh):
    in_specs = (P(("grp", "dev"), None, None), P(("grp", "dev")), P(), P())
    out_specs = (P(("grp", "dev"), None, None), P(("grp", "dev"), None, None))
    return jax.shard_map(body, mesh=mesh, in_specs=in_specs, out_specs=out_specs, check_vma=False)
```

```python
import jax
import jax.numpy as jnp
from jax import lax
from jax.experimental import pallas as pl
from jax.experimental.pallas import tpu as pltpu
from jax.sharding import PartitionSpec as P

DH = 128
QL = 1536
KL = 512
D = 7168
HEADS = 128
BLOCKS = 76
SHARE = (QL + KL) // HEADS
STRIP = 512
MESH = pl.DeviceIdType.MESH

ROUTES = ((0, 1, 2), (1, 2, 0), (2, 0, 1))
STARTS = (0, 48, 88)
ROWS = (48, 40, 40)
HOPS = (2, 1, 3)


def position():
    dev = lax.axis_index("dev")
    return (lax.axis_index("grp"), dev // 8, (dev // 2) % 4, dev % 2)


def device(coords, core):
    x, z, y = coords
    return (x, z * 8 + y * 2 + core)


def shifted(coords, dim, by):
    moved = list(coords)
    moved[dim] = (moved[dim] + by) % 4
    return moved


def exchange_kernel(
    flat_hbm, gains_hbm, place_hbm, serve_hbm,
    got0, got1, got2, gain_out, where_out,
    gain, where, flat0, flat1, flat2, gains_ref, place_ref, serve_ref, tab_v, tab_s,
    own0, own1, own2, first0, first1, first2, second0, second1, second2, gather,
    load_sem, tab_sem, out_sem, first_sem, second_sem, got_sem, gain_sem,
    sent_first, sent_second, sent_got, sent_core, sent_gain,
):
    x, z, y, core = position()
    here = (x, z, y)
    me = x * 32 + z * 8 + y * 2 + core
    flat, own, first, second, got = (
        (flat0, flat1, flat2), (own0, own1, own2), (first0, first1, first2), (second0, second1, second2),
        (got0, got1, got2))

    loads = [
        pltpu.make_async_copy(src, dst, load_sem.at[n]) for n, (src, dst) in enumerate((
            (place_hbm, place_ref), (serve_hbm, serve_ref), (gains_hbm, gains_ref)) + tuple(
            (flat_hbm.at[:, pl.ds(start, n)], part)
            for start, n, part in zip(STARTS, ROWS, flat)))]
    for load in loads:
        load.start()

    barrier = pltpu.get_barrier_semaphore()
    peers = [device(here, 1 - core)]
    for dim in range(3):
        for hop in HOPS:
            for c in (core, 1 - core):
                peers.append(device(shifted(here, dim, hop), c))
    for peer in peers:
        pl.semaphore_signal(barrier, inc=1, device_id=peer, device_id_type=MESH)

    for load in loads[:3]:
        load.wait()
    place = place_ref[...]
    local = place - me * BLOCKS
    held = (local >= 0) & (local < BLOCKS)
    block_of_head = jnp.sum(jnp.where(held, local, 0), axis=0, keepdims=True)
    pairs = jnp.broadcast_to(serve_ref[...] * 128 + block_of_head, (HEADS, HEADS))
    pairs = jnp.transpose(pairs)
    target = lax.broadcasted_iota(jnp.int32, (HEADS, HEADS), 1)
    tab_v[...] = jnp.sum(
        jnp.where(pairs >> 7 == target, pairs & 127, 0), axis=0, keepdims=True)
    table = pltpu.make_async_copy(tab_v, tab_s, tab_sem)
    table.start()
    gather[x, z, y, core] = jnp.concatenate(
        [gains_ref[...], jnp.zeros((1, DH - SHARE), jnp.float32)], axis=1)
    table.wait()

    def pack(o, r, q):
        d1, d2, d3 = ROUTES[o]
        dst = own[o].at[r - 1, q] if r else first[o].at[0, q]
        to = [None] * 3
        to[d1], to[d2] = (here[d1] + r) % 4, (here[d2] + q) % 4
        for b in range(4):
            to[d3] = (here[d3] + b) % 4
            for c in range(2):
                block = tab_s[0, to[0] * 32 + to[1] * 8 + to[2] * 2 + c]
                dst[b, c] = flat[o][block]

    def send(src, dst, sent, landed, to):
        pltpu.make_async_remote_copy(
            src, dst, sent, landed, device_id=to, device_id_type=MESH).start()

    def await_bytes(ref, sem):
        pltpu.make_async_copy(ref, ref, sem).wait()

    for r in HOPS:
        for o in range(3):
            if r == HOPS[0]:
                loads[3 + o].wait()
            for q in range(4):
                pack(o, r, q)
            if (o, r) == (0, HOPS[0]):
                pl.semaphore_wait(barrier, len(peers))
            send(own[o].at[r - 1], first[o].at[r], sent_first.at[o], first_sem.at[o, r - 1],
                 device(shifted(here, ROUTES[o][0], r), core))
    mine = gather.at[x, z, y, core]
    for r in HOPS:
        send(mine, mine, sent_gain.at[0], gain_sem.at[0], device(shifted(here, 0, r), core))

    def forward(o, q):
        d2 = ROUTES[o][1]
        for r in HOPS:
            send(first[o].at[q, r], second[o].at[r - 1, q], sent_second.at[o],
                 second_sem.at[o, r - 1], device(shifted(here, d2, r), core))

    for o in range(3):
        for q in range(4):
            pack(o, 0, q)
        forward(o, 0)

    wanted = jnp.sum(jnp.where(serve_ref[...] == me, place_ref[...], 0), axis=1, keepdims=True)
    wanted = jnp.transpose(jnp.broadcast_to(wanted, (BLOCKS, HEADS)))[:1]
    source = (wanted * 55189) >> 22
    away = ((x - (source >> 5)) & 3, (z - (source >> 3)) & 3, (y - (source >> 1)) & 3)
    for o, (d1, d2, d3) in enumerate(ROUTES):
        slot = ((away[d3] * 2 + (source & 1)) * 4 + away[d2]) * 4 + away[d1]
        where[pl.ds(o, 1), pl.ds(0, BLOCKS)] = slot
    where_copy = pltpu.make_async_copy(where, where_out, out_sem.at[0])
    where_copy.start()

    for q in HOPS:
        for o in range(3):
            await_bytes(first[o].at[q], first_sem.at[o, q - 1])
            forward(o, q)

    await_bytes(gather.at[0, 0, pl.ds(0, 3), 0], gain_sem.at[0])
    mine = gather.at[:, z, y, core]
    for r in HOPS:
        send(mine, mine, sent_gain.at[1], gain_sem.at[1], device(shifted(here, 1, r), core))

    def deliver(o, src, q):
        d3 = ROUTES[o][2]
        for r in HOPS + (0,):
            for c in (0, 1):
                to_core = (core + c) % 2
                a, b = src.at[:, r, to_core], got[o].at[r, core, q]
                if r == 0 and c == 0:
                    pltpu.make_async_copy(a, b, got_sem.at[o]).start()
                else:
                    send(a, b, sent_got.at[o] if r else sent_core.at[o], got_sem.at[o],
                         device(shifted(here, d3, r), to_core))

    for o in range(3):
        deliver(o, first[o].at[:, 0], 0)

    await_bytes(gather.at[pl.ds(0, 3), 0, :, 0], gain_sem.at[1])
    mine = gather.at[:, :, y, core]
    for r in (1, 3, 2, 0):
        for c in (0, 1):
            if r or c:
                n = 2 if r else 3
                send(mine, mine, sent_gain.at[n], gain_sem.at[n],
                     device(shifted(here, 2, r), (core + c) % 2))

    def finish(q):
        for o in range(3):
            await_bytes(second[o].at[q - 1], second_sem.at[o, q - 1])
            deliver(o, second[o].at[q - 1], q)

    finish(HOPS[0])
    finish(HOPS[1])
    rest = gather.at[:, :, pl.ds(0, 3)]
    await_bytes(rest, gain_sem.at[2])
    await_bytes(gather.at[:, :, 3, 0], gain_sem.at[3])
    turned = jnp.transpose(gather[...].reshape(HEADS, HEADS))
    for d in range(HEADS):
        gain[pl.ds(d * SHARE, SHARE)] = jnp.broadcast_to(
            turned[:SHARE, d:d + 1], (SHARE, DH))
    gain_copy = pltpu.make_async_copy(gain, gain_out, out_sem.at[1])
    gain_copy.start()
    finish(HOPS[2])

    where_copy.wait()
    gain_copy.wait()
    for o in range(3):
        await_bytes(got[o], got_sem.at[o])
    for o in range(3):
        await_bytes(first[o].at[pl.ds(1, 3)], sent_first.at[o])
        await_bytes(second[o], sent_second.at[o])
        await_bytes(got[o].at[pl.ds(1, 3)], sent_got.at[o])
        await_bytes(got[o].at[0, 0], sent_core.at[o])
    await_bytes(gather.at[0, 0, pl.ds(0, 3), 0], sent_gain.at[0])
    await_bytes(gather.at[pl.ds(0, 3), 0, :, 0], sent_gain.at[1])
    await_bytes(rest, sent_gain.at[2])
    await_bytes(gather.at[:, :, 3, 0], sent_gain.at[3])


def exchange(flat_master, gains, place, serve_rank):
    def parts(*lead):
        return [pltpu.VMEM(lead + (n, DH), jnp.float32) for n in ROWS]

    dma = pltpu.SemaphoreType.DMA
    return pl.pallas_call(
        exchange_kernel,
        out_shape=parts(4, 2, 4, 4) + [
            pltpu.VMEM((QL + KL, DH), jnp.float32),
            pltpu.VMEM((8, 128), jnp.int32)],
        in_specs=[pl.BlockSpec(memory_space=pltpu.HBM)] * 4,
        out_specs=[pl.BlockSpec(memory_space=pl.ANY)] * 5,
        scratch_shapes=[
            pltpu.VMEM((QL + KL, DH), jnp.float32),
            pltpu.VMEM((8, 128), jnp.int32),
            *parts(BLOCKS),
            pltpu.VMEM((1, SHARE), jnp.float32),
            pltpu.VMEM((BLOCKS, HEADS), jnp.int32),
            pltpu.VMEM((1, HEADS), jnp.int32),
            pltpu.VMEM((1, HEADS), jnp.int32),
            pltpu.SMEM((1, HEADS), jnp.int32),
            *parts(3, 4, 4, 2), *parts(4, 4, 4, 2), *parts(3, 4, 4, 2),
            pltpu.VMEM((4, 4, 4, 2, 1, DH), jnp.float32),
            dma((6,)), dma, dma((2,)), dma((3, 3)), dma((3, 3)), dma((3,)), dma((4,)),
            dma((3,)), dma((3,)), dma((3,)), dma((3,)), dma((4,)),
        ],
        compiler_params=pltpu.CompilerParams(
            collective_id=0, has_side_effects=True, vmem_limit_bytes=52 << 20),
        name="exchange",
    )(flat_master, gains, place, serve_rank)


def split(a):
    high = a.astype(jnp.bfloat16)
    return high, (a - high.astype(jnp.float32)).astype(jnp.bfloat16)


def product_kernel(where, got0, got1, got2, gain, qk_hbm, vo_hbm, uv, uk, qk, vo, sems):
    def block(j):
        return jnp.concatenate(
            [got[where[o, j]] for o, got in enumerate((got0, got1, got2))], axis=0)

    copies = []

    def write(src, dst):
        copy = pltpu.make_async_copy(src, dst, sems.at[len(copies)])
        copy.start()
        copies.append(copy)

    for b in range(KL // DH):
        rows = pl.ds(b * DH, DH)
        g = gain[pl.ds(QL + b * DH, DH)]
        high, low = split(block((QL + KL) // DH + b) * g)
        uv[rows] = jnp.concatenate([high, low, high], axis=1)
        high, low = split(jnp.transpose(block(QL // DH + b) * g))
        uk[:, rows] = jnp.concatenate([high, high, low], axis=0)

    for start in range(0, D, STRIP):
        for column in range(start, start + STRIP, 2 * DH):
            j = (QL + 2 * KL + column) // DH
            (high0, low0), (high1, low1) = split(block(j)), split(block(j + 1))
            high = jnp.concatenate([high0, high1], axis=1)
            low = jnp.concatenate([low0, low1], axis=1)
            out = jnp.dot(
                uv[...], jnp.concatenate([high, high, low], axis=0),
                preferred_element_type=jnp.float32)
            vo[:, pl.ds(column, 2 * DH)] = out.astype(jnp.bfloat16)
        strip = pl.ds(start, STRIP)
        write(vo.at[:, strip], vo_hbm.at[0, :, strip])

    for start in range(0, QL, KL):
        left = []
        for row in range(start, start + KL, DH):
            high, low = split(block(row // DH) * gain[pl.ds(row, DH)])
            left.append(jnp.concatenate([high, low, high], axis=1))
        left = jnp.concatenate(left, axis=0)
        rows = pl.ds(start, KL)
        for column in range(0, KL, 2 * DH):
            out = jnp.dot(
                left, uk[:, pl.ds(column, 2 * DH)], preferred_element_type=jnp.float32)
            qk[rows, pl.ds(column, 2 * DH)] = out.astype(jnp.bfloat16)
        write(qk.at[rows], qk_hbm.at[0, rows])

    for copy in copies:
        copy.wait()


def products(where, got, gain):
    return pl.pallas_call(
        product_kernel,
        in_specs=[pl.BlockSpec(memory_space=pltpu.SMEM)]
        + [pl.BlockSpec(memory_space=pltpu.VMEM)] * 4,
        out_specs=[pl.BlockSpec(memory_space=pl.ANY)] * 2,
        scratch_shapes=[
            pltpu.VMEM((KL, 3 * DH), jnp.bfloat16),
            pltpu.VMEM((3 * DH, KL), jnp.bfloat16),
            pltpu.VMEM((QL, KL), jnp.bfloat16),
            pltpu.VMEM((KL, D), jnp.bfloat16),
            pltpu.SemaphoreType.DMA((D // STRIP + QL // KL,)),
        ],
        out_shape=[
            jax.ShapeDtypeStruct((1, QL, KL), jnp.bfloat16),
            jax.ShapeDtypeStruct((1, KL, D), jnp.bfloat16)],
        compiler_params=pltpu.CompilerParams(vmem_limit_bytes=32 << 20),
        name="products",
    )(where, *got, gain)


def body(flat_master, norm_gains, place, serve_rank):
    *got, gain, where = exchange(flat_master, norm_gains[None], place.T, serve_rank[None])
    got = [g.reshape(HEADS, n, DH) for g, n in zip(got, ROWS)]
    return tuple(products(where, got, gain))


def solution(mesh):
    in_specs = (P(("grp", "dev"), None, None), P(("grp", "dev")), P(), P())
    out_specs = (P(("grp", "dev"), None, None), P(("grp", "dev"), None, None))
    return jax.shard_map(body, mesh=mesh, in_specs=in_specs, out_specs=out_specs, check_vma=False)
```

```python
import jax
import jax.numpy as jnp
from jax import lax
from jax.experimental import pallas as pl
from jax.experimental.pallas import tpu as pltpu
from jax.sharding import PartitionSpec as P

DH = 128
QL = 1536
KL = 512
D = 7168
HEADS = 128
BLOCKS = 76
SHARE = (QL + KL) // HEADS
STRIP = 512
MESH = pl.DeviceIdType.MESH

ROUTES = ((0, 1, 2), (1, 2, 0), (2, 0, 1))
STARTS = (0, 48, 88)
ROWS = (48, 40, 40)
HOPS = (2, 1, 3)


def position():
    dev = lax.axis_index("dev")
    return (lax.axis_index("grp"), dev // 8, (dev // 2) % 4, dev % 2)


def device(coords, core):
    x, z, y = coords
    return (x, z * 8 + y * 2 + core)


def shifted(coords, dim, by):
    moved = list(coords)
    moved[dim] = (moved[dim] + by) % 4
    return moved


def exchange_kernel(
    flat_hbm, gains_hbm, place_hbm, serve_hbm,
    got0, got1, got2, gain_out, where_out,
    gain, where, flat0, flat1, flat2, gains_ref, place_ref, serve_ref, tab_v, tab_s,
    own0, own1, own2, first0, first1, first2, second0, second1, second2, gather,
    load_sem, tab_sem, out_sem, first_sem, second_sem, got_sem, gain_sem,
    sent_first, sent_second, sent_got, sent_core, sent_gain,
):
    x, z, y, core = position()
    here = (x, z, y)
    me = x * 32 + z * 8 + y * 2 + core
    flat, own, first, second, got = (
        (flat0, flat1, flat2), (own0, own1, own2), (first0, first1, first2), (second0, second1, second2),
        (got0, got1, got2))

    loads = [
        pltpu.make_async_copy(src, dst, load_sem.at[n]) for n, (src, dst) in enumerate((
            (place_hbm, place_ref), (serve_hbm, serve_ref), (gains_hbm, gains_ref)) + tuple(
            (flat_hbm.at[:, pl.ds(start, n)], part)
            for start, n, part in zip(STARTS, ROWS, flat)))]
    for load in loads:
        load.start()

    barrier = pltpu.get_barrier_semaphore()
    peers = [device(here, 1 - core)]
    for dim in range(3):
        for hop in HOPS:
            for c in (core, 1 - core):
                peers.append(device(shifted(here, dim, hop), c))
    for peer in peers:
        pl.semaphore_signal(barrier, inc=1, device_id=peer, device_id_type=MESH)

    for load in loads[:3]:
        load.wait()
    place = place_ref[...]
    local = place - me * BLOCKS
    held = (local >= 0) & (local < BLOCKS)
    block_of_head = jnp.sum(jnp.where(held, local, 0), axis=0, keepdims=True)
    pairs = jnp.broadcast_to(serve_ref[...] * 128 + block_of_head, (HEADS, HEADS))
    pairs = jnp.transpose(pairs)
    target = lax.broadcasted_iota(jnp.int32, (HEADS, HEADS), 1)
    tab_v[...] = jnp.sum(
        jnp.where(pairs >> 7 == target, pairs & 127, 0), axis=0, keepdims=True)
    table = pltpu.make_async_copy(tab_v, tab_s, tab_sem)
    table.start()
    gather[x, z, y, core] = jnp.concatenate(
        [gains_ref[...], jnp.zeros((1, DH - SHARE), jnp.float32)], axis=1)
    table.wait()

    def pack(o, r, q):
        d1, d2, d3 = ROUTES[o]
        dst = own[o].at[r - 1, q] if r else first[o].at[0, q]
        to = [None] * 3
        to[d1], to[d2] = (here[d1] + r) % 4, (here[d2] + q) % 4
        for b in range(4):
            to[d3] = (here[d3] + b) % 4
            for c in range(2):
                block = tab_s[0, to[0] * 32 + to[1] * 8 + to[2] * 2 + c]
                dst[b, c] = flat[o][block]

    def send(src, dst, sent, landed, to):
        pltpu.make_async_remote_copy(
            src, dst, sent, landed, device_id=to, device_id_type=MESH).start()

    def await_bytes(ref, sem):
        pltpu.make_async_copy(ref, ref, sem).wait()

    for r in HOPS:
        for o in range(3):
            if r == HOPS[0]:
                loads[3 + o].wait()
            for q in range(4):
                pack(o, r, q)
            if (o, r) == (0, HOPS[0]):
                pl.semaphore_wait(barrier, len(peers))
            send(own[o].at[r - 1], first[o].at[r], sent_first.at[o], first_sem.at[o, r - 1],
                 device(shifted(here, ROUTES[o][0], r), core))
    mine = gather.at[x, z, y, core]
    for r in HOPS:
        send(mine, mine, sent_gain.at[0], gain_sem.at[0], device(shifted(here, 0, r), core))

    def forward(o, q):
        d2 = ROUTES[o][1]
        for r in HOPS:
            send(first[o].at[q, r], second[o].at[r - 1, q], sent_second.at[o],
                 second_sem.at[o, r - 1], device(shifted(here, d2, r), core))

    for o in range(3):
        for q in range(4):
            pack(o, 0, q)
        forward(o, 0)

    wanted = jnp.sum(jnp.where(serve_ref[...] == me, place_ref[...], 0), axis=1, keepdims=True)
    wanted = jnp.transpose(jnp.broadcast_to(wanted, (BLOCKS, HEADS)))[:1]
    source = (wanted * 55189) >> 22
    away = ((x - (source >> 5)) & 3, (z - (source >> 3)) & 3, (y - (source >> 1)) & 3)
    for o, (d1, d2, d3) in enumerate(ROUTES):
        slot = ((away[d3] * 2 + (source & 1)) * 4 + away[d2]) * 4 + away[d1]
        where[pl.ds(o, 1), pl.ds(0, BLOCKS)] = slot
    where_copy = pltpu.make_async_copy(where, where_out, out_sem.at[0])
    where_copy.start()

    for q in HOPS:
        for o in range(3):
            await_bytes(first[o].at[q], first_sem.at[o, q - 1])
            forward(o, q)

    await_bytes(gather.at[0, 0, pl.ds(0, 3), 0], gain_sem.at[0])
    mine = gather.at[:, z, y, core]
    for r in HOPS:
        send(mine, mine, sent_gain.at[1], gain_sem.at[1], device(shifted(here, 1, r), core))

    def deliver(o, src, q):
        d3 = ROUTES[o][2]
        for r in HOPS + (0,):
            for c in (0, 1):
                to_core = (core + c) % 2
                a, b = src.at[:, r, to_core], got[o].at[r, core, q]
                if r == 0 and c == 0:
                    pltpu.make_async_copy(a, b, got_sem.at[o]).start()
                else:
                    send(a, b, sent_got.at[o] if r else sent_core.at[o], got_sem.at[o],
                         device(shifted(here, d3, r), to_core))

    for o in range(3):
        deliver(o, first[o].at[:, 0], 0)

    await_bytes(gather.at[pl.ds(0, 3), 0, :, 0], gain_sem.at[1])
    mine = gather.at[:, :, y, core]
    for r in HOPS:
        send(mine, mine, sent_gain.at[2], gain_sem.at[2], device(shifted(here, 2, r), core))

    def finish(q):
        for o in range(3):
            await_bytes(second[o].at[q - 1], second_sem.at[o, q - 1])
            deliver(o, second[o].at[q - 1], q)

    finish(HOPS[0])
    await_bytes(gather.at[:, :, pl.ds(0, 3), 0], gain_sem.at[2])
    mine = gather.at[:, :, :, core]
    send(mine, mine, sent_gain.at[3], gain_sem.at[3], device(here, 1 - core))
    finish(HOPS[1])
    await_bytes(gather.at[:, :, :, 0], gain_sem.at[3])
    turned = jnp.transpose(gather[...].reshape(HEADS, HEADS))
    for d in range(HEADS):
        gain[pl.ds(d * SHARE, SHARE)] = jnp.broadcast_to(
            turned[:SHARE, d:d + 1], (SHARE, DH))
    gain_copy = pltpu.make_async_copy(gain, gain_out, out_sem.at[1])
    gain_copy.start()
    finish(HOPS[2])

    where_copy.wait()
    gain_copy.wait()
    for o in range(3):
        await_bytes(got[o], got_sem.at[o])
    for o in range(3):
        await_bytes(first[o].at[pl.ds(1, 3)], sent_first.at[o])
        await_bytes(second[o], sent_second.at[o])
        await_bytes(got[o].at[pl.ds(1, 3)], sent_got.at[o])
        await_bytes(got[o].at[0, 0], sent_core.at[o])
    await_bytes(gather.at[0, 0, pl.ds(0, 3), 0], sent_gain.at[0])
    await_bytes(gather.at[pl.ds(0, 3), 0, :, 0], sent_gain.at[1])
    await_bytes(gather.at[:, :, pl.ds(0, 3), 0], sent_gain.at[2])
    await_bytes(gather.at[:, :, :, 0], sent_gain.at[3])


def exchange(flat_master, gains, place, serve_rank):
    def parts(*lead):
        return [pltpu.VMEM(lead + (n, DH), jnp.float32) for n in ROWS]

    dma = pltpu.SemaphoreType.DMA
    return pl.pallas_call(
        exchange_kernel,
        out_shape=parts(4, 2, 4, 4) + [
            pltpu.VMEM((QL + KL, DH), jnp.float32),
            pltpu.VMEM((8, 128), jnp.int32)],
        in_specs=[pl.BlockSpec(memory_space=pltpu.HBM)] * 4,
        out_specs=[pl.BlockSpec(memory_space=pl.ANY)] * 5,
        scratch_shapes=[
            pltpu.VMEM((QL + KL, DH), jnp.float32),
            pltpu.VMEM((8, 128), jnp.int32),
            *parts(BLOCKS),
            pltpu.VMEM((1, SHARE), jnp.float32),
            pltpu.VMEM((BLOCKS, HEADS), jnp.int32),
            pltpu.VMEM((1, HEADS), jnp.int32),
            pltpu.VMEM((1, HEADS), jnp.int32),
            pltpu.SMEM((1, HEADS), jnp.int32),
            *parts(3, 4, 4, 2), *parts(4, 4, 4, 2), *parts(3, 4, 4, 2),
            pltpu.VMEM((4, 4, 4, 2, 1, DH), jnp.float32),
            dma((6,)), dma, dma((2,)), dma((3, 3)), dma((3, 3)), dma((3,)), dma((4,)),
            dma((3,)), dma((3,)), dma((3,)), dma((3,)), dma((4,)),
        ],
        compiler_params=pltpu.CompilerParams(
            collective_id=0, has_side_effects=True, vmem_limit_bytes=52 << 20),
        name="exchange",
    )(flat_master, gains, place, serve_rank)


def split(a):
    high = a.astype(jnp.bfloat16)
    return high, (a - high.astype(jnp.float32)).astype(jnp.bfloat16)


def product_kernel(where, got0, got1, got2, gain, qk_hbm, vo_hbm, uv, uk, qk, vo, sems):
    def block(j):
        return jnp.concatenate(
            [got[where[o, j]] for o, got in enumerate((got0, got1, got2))], axis=0)

    copies = []

    def write(src, dst):
        copy = pltpu.make_async_copy(src, dst, sems.at[len(copies)])
        copy.start()
        copies.append(copy)

    for b in range(KL // DH):
        rows = pl.ds(b * DH, DH)
        g = gain[pl.ds(QL + b * DH, DH)]
        high, low = split(block((QL + KL) // DH + b) * g)
        uv[rows] = jnp.concatenate([high, low, high], axis=1)

    for start in range(0, D, STRIP):
        for column in range(start, start + STRIP, 2 * DH):
            j = (QL + 2 * KL + column) // DH
            (high0, low0), (high1, low1) = split(block(j)), split(block(j + 1))
            high = jnp.concatenate([high0, high1], axis=1)
            low = jnp.concatenate([low0, low1], axis=1)
            out = jnp.dot(
                uv[...], jnp.concatenate([high, high, low], axis=0),
                preferred_element_type=jnp.float32)
            vo[:, pl.ds(column, 2 * DH)] = out.astype(jnp.bfloat16)
        strip = pl.ds(start, STRIP)
        write(vo.at[:, strip], vo_hbm.at[0, :, strip])

    for b in range(KL // DH):
        g = gain[pl.ds(QL + b * DH, DH)]
        high, low = split(jnp.transpose(block(QL // DH + b) * g))
        uk[:, pl.ds(b * DH, DH)] = jnp.concatenate([high, high, low], axis=0)
    for start in range(0, QL, KL):
        left = []
        for row in range(start, start + KL, DH):
            high, low = split(block(row // DH) * gain[pl.ds(row, DH)])
            left.append(jnp.concatenate([high, low, high], axis=1))
        left = jnp.concatenate(left, axis=0)
        rows = pl.ds(start, KL)
        for column in range(0, KL, 2 * DH):
            out = jnp.dot(
                left, uk[:, pl.ds(column, 2 * DH)], preferred_element_type=jnp.float32)
            qk[rows, pl.ds(column, 2 * DH)] = out.astype(jnp.bfloat16)
        write(qk.at[rows], qk_hbm.at[0, rows])

    for copy in copies:
        copy.wait()


def products(where, got, gain):
    return pl.pallas_call(
        product_kernel,
        in_specs=[pl.BlockSpec(memory_space=pltpu.SMEM)]
        + [pl.BlockSpec(memory_space=pltpu.VMEM)] * 4,
        out_specs=[pl.BlockSpec(memory_space=pl.ANY)] * 2,
        scratch_shapes=[
            pltpu.VMEM((KL, 3 * DH), jnp.bfloat16),
            pltpu.VMEM((3 * DH, KL), jnp.bfloat16),
            pltpu.VMEM((QL, KL), jnp.bfloat16),
            pltpu.VMEM((KL, D), jnp.bfloat16),
            pltpu.SemaphoreType.DMA((D // STRIP + QL // KL,)),
        ],
        out_shape=[
            jax.ShapeDtypeStruct((1, QL, KL), jnp.bfloat16),
            jax.ShapeDtypeStruct((1, KL, D), jnp.bfloat16)],
        compiler_params=pltpu.CompilerParams(vmem_limit_bytes=32 << 20),
        name="products",
    )(where, *got, gain)


def body(flat_master, norm_gains, place, serve_rank):
    *got, gain, where = exchange(flat_master, norm_gains[None], place.T, serve_rank[None])
    got = [g.reshape(HEADS, n, DH) for g, n in zip(got, ROWS)]
    return tuple(products(where, got, gain))


def solution(mesh):
    in_specs = (P(("grp", "dev"), None, None), P(("grp", "dev")), P(), P())
    out_specs = (P(("grp", "dev"), None, None), P(("grp", "dev"), None, None))
    return jax.shard_map(body, mesh=mesh, in_specs=in_specs, out_specs=out_specs, check_vma=False)
```

```python
import jax
import jax.numpy as jnp
from jax import lax
from jax.experimental import pallas as pl
from jax.experimental.pallas import tpu as pltpu
from jax.sharding import PartitionSpec as P

DH = 128
QL = 1536
KL = 512
D = 7168
HEADS = 128
BLOCKS = 76
SHARE = (QL + KL) // HEADS
STRIP = 512
MESH = pl.DeviceIdType.MESH

ROUTES = ((0, 1, 2), (1, 2, 0), (2, 0, 1))
STARTS = (0, 48, 88)
ROWS = (48, 40, 40)
HOPS = (2, 1, 3)


def position():
    dev = lax.axis_index("dev")
    return (lax.axis_index("grp"), dev // 8, (dev // 2) % 4, dev % 2)


def device(coords, core):
    x, z, y = coords
    return (x, z * 8 + y * 2 + core)


def shifted(coords, dim, by):
    moved = list(coords)
    moved[dim] = (moved[dim] + by) % 4
    return moved


def exchange_kernel(
    flat_hbm, gains_hbm, place_hbm, serve_hbm,
    got0, got1, got2, gain_out, where_out,
    gain, where, flat0, flat1, flat2, gains_ref, place_ref, serve_ref, tab_v, tab_s,
    own0, own1, own2, first0, first1, first2, second0, second1, second2, gather,
    load_sem, tab_sem, out_sem, first_sem, second_sem, got_sem, gain_sem,
    sent_first, sent_second, sent_got, sent_core, sent_gain,
):
    x, z, y, core = position()
    here = (x, z, y)
    me = x * 32 + z * 8 + y * 2 + core
    flat, own, first, second, got = (
        (flat0, flat1, flat2), (own0, own1, own2), (first0, first1, first2), (second0, second1, second2),
        (got0, got1, got2))

    loads = [
        pltpu.make_async_copy(src, dst, load_sem.at[n]) for n, (src, dst) in enumerate((
            (place_hbm, place_ref), (serve_hbm, serve_ref), (gains_hbm, gains_ref)) + tuple(
            (flat_hbm.at[:, pl.ds(start, n)], part)
            for start, n, part in zip(STARTS, ROWS, flat)))]
    for load in loads:
        load.start()

    barrier = pltpu.get_barrier_semaphore()
    peers = [device(here, 1 - core)]
    for dim in range(3):
        for hop in HOPS:
            for c in (core, 1 - core):
                peers.append(device(shifted(here, dim, hop), c))
    for peer in peers:
        pl.semaphore_signal(barrier, inc=1, device_id=peer, device_id_type=MESH)

    for load in loads[:3]:
        load.wait()
    place = place_ref[...]
    local = place - me * BLOCKS
    held = (local >= 0) & (local < BLOCKS)
    block_of_head = jnp.sum(jnp.where(held, local, 0), axis=0, keepdims=True)
    pairs = jnp.broadcast_to(serve_ref[...] * 128 + block_of_head, (HEADS, HEADS))
    pairs = jnp.transpose(pairs)
    target = lax.broadcasted_iota(jnp.int32, (HEADS, HEADS), 1)
    tab_v[...] = jnp.sum(
        jnp.where(pairs >> 7 == target, pairs & 127, 0), axis=0, keepdims=True)
    table = pltpu.make_async_copy(tab_v, tab_s, tab_sem)
    table.start()
    gather[x, z, y, core] = jnp.concatenate(
        [gains_ref[...], jnp.zeros((1, DH - SHARE), jnp.float32)], axis=1)
    table.wait()

    def pack(o, r, q):
        d1, d2, d3 = ROUTES[o]
        dst = own[o].at[r - 1, q] if r else first[o].at[0, q]
        to = [None] * 3
        to[d1], to[d2] = (here[d1] + r) % 4, (here[d2] + q) % 4
        for b in range(4):
            to[d3] = (here[d3] + b) % 4
            for c in range(2):
                block = tab_s[0, to[0] * 32 + to[1] * 8 + to[2] * 2 + c]
                dst[b, c] = flat[o][block]

    def send(src, dst, sent, landed, to):
        pltpu.make_async_remote_copy(
            src, dst, sent, landed, device_id=to, device_id_type=MESH).start()

    def await_bytes(ref, sem):
        pltpu.make_async_copy(ref, ref, sem).wait()

    for r in HOPS:
        for o in range(3):
            if r == HOPS[0]:
                loads[3 + o].wait()
            for q in range(4):
                pack(o, r, q)
            if (o, r) == (0, HOPS[0]):
                pl.semaphore_wait(barrier, len(peers))
            send(own[o].at[r - 1], first[o].at[r], sent_first.at[o], first_sem.at[o, r - 1],
                 device(shifted(here, ROUTES[o][0], r), core))
    mine = gather.at[x, z, y, core]
    for r in HOPS:
        send(mine, mine, sent_gain.at[0], gain_sem.at[0], device(shifted(here, 0, r), core))

    def forward(o, q):
        d2 = ROUTES[o][1]
        for r in HOPS:
            send(first[o].at[q, r], second[o].at[r - 1, q], sent_second.at[o],
                 second_sem.at[o, r - 1], device(shifted(here, d2, r), core))

    for o in range(3):
        for q in range(4):
            pack(o, 0, q)
        forward(o, 0)

    wanted = jnp.sum(jnp.where(serve_ref[...] == me, place_ref[...], 0), axis=1, keepdims=True)
    wanted = jnp.transpose(jnp.broadcast_to(wanted, (BLOCKS, HEADS)))[:1]
    source = (wanted * 55189) >> 22
    away = ((x - (source >> 5)) & 3, (z - (source >> 3)) & 3, (y - (source >> 1)) & 3)
    for o, (d1, d2, d3) in enumerate(ROUTES):
        slot = ((away[d3] * 2 + (source & 1)) * 4 + away[d2]) * 4 + away[d1]
        where[pl.ds(o, 1), pl.ds(0, BLOCKS)] = slot
    where_copy = pltpu.make_async_copy(where, where_out, out_sem.at[0])
    where_copy.start()

    for q in HOPS:
        for o in range(3):
            await_bytes(first[o].at[q], first_sem.at[o, q - 1])
            forward(o, q)

    await_bytes(gather.at[0, 0, pl.ds(0, 3), 0], gain_sem.at[0])
    mine = gather.at[:, z, y, core]
    for r in HOPS:
        send(mine, mine, sent_gain.at[1], gain_sem.at[1], device(shifted(here, 1, r), core))

    def deliver(o, src, q):
        d3 = ROUTES[o][2]
        for r in HOPS + (0,):
            for c in (0, 1):
                to_core = (core + c) % 2
                a, b = src.at[:, r, to_core], got[o].at[r, core, q]
                if r == 0 and c == 0:
                    pltpu.make_async_copy(a, b, got_sem.at[o]).start()
                else:
                    send(a, b, sent_got.at[o] if r else sent_core.at[o], got_sem.at[o],
                         device(shifted(here, d3, r), to_core))

    for o in range(3):
        deliver(o, first[o].at[:, 0], 0)

    await_bytes(gather.at[pl.ds(0, 3), 0, :, 0], gain_sem.at[1])
    mine = gather.at[:, :, y, core]
    for r in HOPS:
        send(mine, mine, sent_gain.at[2], gain_sem.at[2], device(shifted(here, 2, r), core))

    def finish(q):
        for o in range(3):
            await_bytes(second[o].at[q - 1], second_sem.at[o, q - 1])
            deliver(o, second[o].at[q - 1], q)

    finish(HOPS[0])
    await_bytes(gather.at[:, :, pl.ds(0, 3), 0], gain_sem.at[2])
    mine = gather.at[:, :, :, core]
    send(mine, mine, sent_gain.at[3], gain_sem.at[3], device(here, 1 - core))
    finish(HOPS[1])
    await_bytes(gather.at[:, :, :, 0], gain_sem.at[3])
    turned = jnp.transpose(gather[...].reshape(HEADS, HEADS))
    for d in range(HEADS):
        gain[pl.ds(d * SHARE, SHARE)] = jnp.broadcast_to(
            turned[:SHARE, d:d + 1], (SHARE, DH))
    gain_copy = pltpu.make_async_copy(gain, gain_out, out_sem.at[1])
    gain_copy.start()
    finish(HOPS[2])

    where_copy.wait()
    gain_copy.wait()
    for o in range(3):
        await_bytes(got[o], got_sem.at[o])
    for o in range(3):
        await_bytes(first[o].at[pl.ds(1, 3)], sent_first.at[o])
        await_bytes(second[o], sent_second.at[o])
        await_bytes(got[o].at[pl.ds(1, 3)], sent_got.at[o])
        await_bytes(got[o].at[0, 0], sent_core.at[o])
    await_bytes(gather.at[0, 0, pl.ds(0, 3), 0], sent_gain.at[0])
    await_bytes(gather.at[pl.ds(0, 3), 0, :, 0], sent_gain.at[1])
    await_bytes(gather.at[:, :, pl.ds(0, 3), 0], sent_gain.at[2])
    await_bytes(gather.at[:, :, :, 0], sent_gain.at[3])


def exchange(flat_master, gains, place, serve_rank):
    def parts(*lead):
        return [pltpu.VMEM(lead + (n, DH), jnp.float32) for n in ROWS]

    dma = pltpu.SemaphoreType.DMA
    return pl.pallas_call(
        exchange_kernel,
        out_shape=parts(4, 2, 4, 4) + [
            pltpu.VMEM((QL + KL, DH), jnp.float32),
            pltpu.VMEM((8, 128), jnp.int32)],
        in_specs=[pl.BlockSpec(memory_space=pltpu.HBM)] * 4,
        out_specs=[pl.BlockSpec(memory_space=pl.ANY)] * 5,
        scratch_shapes=[
            pltpu.VMEM((QL + KL, DH), jnp.float32),
            pltpu.VMEM((8, 128), jnp.int32),
            *parts(BLOCKS),
            pltpu.VMEM((1, SHARE), jnp.float32),
            pltpu.VMEM((BLOCKS, HEADS), jnp.int32),
            pltpu.VMEM((1, HEADS), jnp.int32),
            pltpu.VMEM((1, HEADS), jnp.int32),
            pltpu.SMEM((1, HEADS), jnp.int32),
            *parts(3, 4, 4, 2), *parts(4, 4, 4, 2), *parts(3, 4, 4, 2),
            pltpu.VMEM((4, 4, 4, 2, 1, DH), jnp.float32),
            dma((6,)), dma, dma((2,)), dma((3, 3)), dma((3, 3)), dma((3,)), dma((4,)),
            dma((3,)), dma((3,)), dma((3,)), dma((3,)), dma((4,)),
        ],
        compiler_params=pltpu.CompilerParams(
            collective_id=0, has_side_effects=True, vmem_limit_bytes=52 << 20),
        name="exchange",
    )(flat_master, gains, place, serve_rank)


def split(a):
    high = a.astype(jnp.bfloat16)
    return high, (a - high.astype(jnp.float32)).astype(jnp.bfloat16)


def product_kernel(where, got0, got1, got2, gain, qk_hbm, vo_hbm, uv, uk, qk, vo, sems):
    def block(j):
        return jnp.concatenate(
            [got[where[o, j]] for o, got in enumerate((got0, got1, got2))], axis=0)

    copies = []

    def write(src, dst):
        copy = pltpu.make_async_copy(src, dst, sems.at[len(copies)])
        copy.start()
        copies.append(copy)

    for b in range(KL // DH):
        rows = pl.ds(b * DH, DH)
        g = gain[pl.ds(QL + b * DH, DH)]
        high, low = split(block((QL + KL) // DH + b) * g)
        uv[rows] = jnp.concatenate([high, low, high], axis=1)

    for start in range(0, D, STRIP):
        for column in range(start, start + STRIP, 2 * DH):
            j = (QL + 2 * KL + column) // DH
            (high0, low0), (high1, low1) = split(block(j)), split(block(j + 1))
            high = jnp.concatenate([high0, high1], axis=1)
            low = jnp.concatenate([low0, low1], axis=1)
            out = jnp.dot(
                uv[:, pl.ds(0, 2 * DH)], jnp.concatenate([high, high], axis=0),
                preferred_element_type=jnp.float32)
            out += jnp.dot(uv[:, pl.ds(2 * DH, DH)], low, preferred_element_type=jnp.float32)
            vo[:, pl.ds(column, 2 * DH)] = out.astype(jnp.bfloat16)
        strip = pl.ds(start, STRIP)
        write(vo.at[:, strip], vo_hbm.at[0, :, strip])

    for b in range(KL // DH):
        g = gain[pl.ds(QL + b * DH, DH)]
        high, low = split(jnp.transpose(block(QL // DH + b) * g))
        uk[:, pl.ds(b * DH, DH)] = jnp.concatenate([high, high, low], axis=0)
    for start in range(0, QL, KL):
        left = []
        for row in range(start, start + KL, DH):
            high, low = split(block(row // DH) * gain[pl.ds(row, DH)])
            left.append(jnp.concatenate([high, low, high], axis=1))
        left = jnp.concatenate(left, axis=0)
        rows = pl.ds(start, KL)
        for column in range(0, KL, 2 * DH):
            out = jnp.dot(
                left, uk[:, pl.ds(column, 2 * DH)], preferred_element_type=jnp.float32)
            qk[rows, pl.ds(column, 2 * DH)] = out.astype(jnp.bfloat16)
        write(qk.at[rows], qk_hbm.at[0, rows])

    for copy in copies:
        copy.wait()


def products(where, got, gain):
    return pl.pallas_call(
        product_kernel,
        in_specs=[pl.BlockSpec(memory_space=pltpu.SMEM)]
        + [pl.BlockSpec(memory_space=pltpu.VMEM)] * 4,
        out_specs=[pl.BlockSpec(memory_space=pl.ANY)] * 2,
        scratch_shapes=[
            pltpu.VMEM((KL, 3 * DH), jnp.bfloat16),
            pltpu.VMEM((3 * DH, KL), jnp.bfloat16),
            pltpu.VMEM((QL, KL), jnp.bfloat16),
            pltpu.VMEM((KL, D), jnp.bfloat16),
            pltpu.SemaphoreType.DMA((D // STRIP + QL // KL,)),
        ],
        out_shape=[
            jax.ShapeDtypeStruct((1, QL, KL), jnp.bfloat16),
            jax.ShapeDtypeStruct((1, KL, D), jnp.bfloat16)],
        compiler_params=pltpu.CompilerParams(vmem_limit_bytes=32 << 20),
        name="products",
    )(where, *got, gain)


def body(flat_master, norm_gains, place, serve_rank):
    *got, gain, where = exchange(flat_master, norm_gains[None], place.T, serve_rank[None])
    got = [g.reshape(HEADS, n, DH) for g, n in zip(got, ROWS)]
    return tuple(products(where, got, gain))


def solution(mesh):
    in_specs = (P(("grp", "dev"), None, None), P(("grp", "dev")), P(), P())
    out_specs = (P(("grp", "dev"), None, None), P(("grp", "dev"), None, None))
    return jax.shard_map(body, mesh=mesh, in_specs=in_specs, out_specs=out_specs, check_vma=False)
```
